1024 devices in a mesh: ctx: 64 (over y, z), head: 16 (over x, core).
Axes of the slice: x: 8, y: 8, z: 8, core: 2. Of those that a mesh axis runs over, the one named last changes fastest.
Arguments:
- queries: bfloat16 [32768, 4096], P('ctx', 'head'), may hold values from -6 to 6
- keys: bfloat16 [32768, 4096], P('ctx', 'head'), may hold values from -6 to 6
- values: bfloat16 [32768, 4096], P('ctx', 'head'), may hold values from -6 to 6
- out_grad: bfloat16 [32768, 4096], P('ctx', 'head'), may hold values from -6 to 6
- gain: float32 [4096], P('head'), may hold values from 0.5 to 1.5
- doc_lengths: int32 [64], replicated, may hold values from 1 to 8192, 32768 in all
Outputs:
- normed: bfloat16 [32768, 4096], P('ctx', 'head')
- query_grad: bfloat16 [32768, 4096], P('ctx', 'head')
- key_grad: bfloat16 [32768, 4096], P('ctx', 'head')
- value_grad: bfloat16 [32768, 4096], P('ctx', 'head')
The draws below stay inside these ranges and needn't reach their ends.
Inputs may be any that keep to these rules, and one draw needn't show every extreme that they name: `doc_lengths`: 64 document lengths in order; the first document starts at token 0 and the lengths sum to 32768.
All inputs are finite; a program needn't handle non-finite values.
Results may differ from the reference program's by a relative error of at most 0.0053.
Values sent between devices are 32-bit elements; how exact they have to be, the bound alone decides.
No kernel may reach another device: no remote copies, remote signals or barrier semaphores. Data moves between devices by JAX's collectives and lax.ppermute only.
A program may use at most 32 MiB of HBM per device.

```python
import math
import jax
import jax.numpy as jnp
import numpy as np
from jax import lax

HEADS = 32
DH = 128
BLK = 256
TOKENS = 32768
FEAT = 4096
DOCS = 64
LONGEST = 8192


def steps_of(stream_key, extent, cuts, low, largest):
    def one(dim, parts):
        draws = jax.random.uniform(jax.random.fold_in(jax.random.fold_in(stream_key, 6), dim), (parts,), jnp.float32, low / len(cuts), largest / len(cuts))
        return jnp.repeat(jnp.exp(draws), extent[dim] // parts).reshape((-1,) + (1,) * (len(extent) - dim - 1))

    level = one(*cuts[0])
    for cut in cuts[1:]:
        level = level * one(*cut)
    return level


def split_up(amount, total, bound, slope):
    loads = [(1 << 20) // math.isqrt(grade ** slope) + 1 for grade in range(2, amount + 1)]
    surplus, counts = total - bound - (amount - 1), [1] * (amount - 1)
    while surplus > 0:
        free = [i for i in range(amount - 1) if counts[i] < bound]
        pool, budget = sum([loads[i] for i in free]), surplus
        for i in free:
            more = min(bound - counts[i], max(1, budget * loads[i] // pool), surplus)
            counts[i] = counts[i] + more
            surplus = surplus - more
    return np.array([bound] + counts)


def uneven_parts(key, amount, total, most, lean):
    if amount == 2:
        one = jax.random.randint(key, (), max(1, total - most), min(most, total - 1) + 1)
        return jnp.stack([one, total - one])
    sizes = jnp.asarray(split_up(amount, total, most, lean), jnp.int32)
    twos = (amount - 1) // 2
    donor, taker = sizes[1:1 + 2 * twos:2], sizes[2:2 + 2 * twos:2]
    room = jnp.minimum(donor - 1, most - taker)
    passed = jax.random.randint(jax.random.fold_in(key, 1), (twos,), 0, 1 << 20) % (room + 1)
    sizes = sizes.at[1:1 + 2 * twos:2].set(donor - passed).at[2:2 + 2 * twos:2].set(taker + passed)
    return sizes[jax.random.permutation(jax.random.fold_in(key, 2), amount)]


def scatter_about(key, dims, spread, bound, split=(), kind=jnp.bfloat16):
    result = jax.random.normal(key, dims, jnp.float32) * spread
    if len(split) > 0:
        result = steps_of(key, dims, split, -0.22, 0.18) * result
    return jnp.clip(result, min=-bound, max=bound).astype(kind)


def setup_inputs(seed: int = 0) -> dict:
    streams_of = jax.random.split(jax.random.key(seed), 7)
    return {
        "queries": scatter_about(streams_of[0], (TOKENS, FEAT), 1.0, 6.0, ((0, 64), (1, 16))),
        "keys": scatter_about(streams_of[1], (TOKENS, FEAT), 1.0, 6.0, ((0, 64), (1, 16))),
        "values": scatter_about(streams_of[2], (TOKENS, FEAT), 1.0, 6.0, ((0, 64), (1, 16))),
        "out_grad": scatter_about(streams_of[3], (TOKENS, FEAT), 1.0, 6.0, ((0, 64), (1, 16))),
        "gain": jnp.clip(1.0 + 0.1 * jax.random.normal(streams_of[4], (FEAT,), jnp.float32), 0.5, 1.5),
        "doc_lengths": uneven_parts(streams_of[5], DOCS, TOKENS, LONGEST, 2).astype(jnp.int32),
    }


HIGHEST = lax.Precision.HIGHEST
EPSILON = 1e-06

def doc_number(starts, positions):
    hits = (starts[None, :] <= positions[:, None]).astype(jnp.int32)
    return (lax.optimization_barrier(jnp.sum(hits, axis=1)) - 1).astype(jnp.int32)

def masked_scores(left, right, allowed):
    scores = jnp.einsum('thd,shd->hts', left.astype(jnp.float32), right.astype(jnp.float32), precision=HIGHEST)
    return jnp.where(allowed[None], scores, 0.0).astype(jnp.bfloat16)

def reference(queries, keys, values, out_grad, gain, doc_lengths):
    lengths = doc_lengths.astype(jnp.int32)
    starts = (jnp.cumsum(lengths) - lengths).astype(jnp.int32)
    block_total = TOKENS // BLK
    block_shape = (block_total, BLK, HEADS, DH)
    positions = jnp.arange(TOKENS, dtype=jnp.int32)
    doc_tok = doc_number(starts, positions).reshape(block_total, BLK)
    edges = (BLK * jnp.arange(block_total + 1, dtype=jnp.int32)).astype(jnp.int32)
    doc_before = doc_number(starts, edges - 1)
    doc_at = doc_number(starts, edges)
    causal = jnp.arange(BLK)[:, None] >= jnp.arange(BLK)[None, :]
    query_blocks = queries.reshape(block_shape)
    key_blocks = keys.reshape(block_shape)
    value_blocks = values.reshape(block_shape)
    grad_blocks = out_grad.reshape(block_total, BLK, FEAT)

    def forward_step(state, inputs):
        query_block, key_block, value_block, grad_block, block_docs, before, doc_after = inputs
        allowed = causal & (block_docs[:, None] == block_docs[None, :])
        probs = masked_scores(query_block, key_block, allowed)
        apply_in = (block_docs == before).astype(jnp.float32)[:, None, None]
        within = jnp.einsum('hts,shd->thd', probs.astype(jnp.float32), value_block.astype(jnp.float32), precision=HIGHEST)
        across = jnp.einsum('thi,hij->thj', query_block.astype(jnp.float32), state, precision=HIGHEST) * apply_in
        attended = (within + across).reshape(BLK, FEAT)
        scaled_grad = grad_block.astype(jnp.float32) * gain
        radius = jnp.sqrt(lax.optimization_barrier(jnp.sum(attended * attended, axis=1)) / FEAT + EPSILON)
        inner_sum = lax.optimization_barrier(jnp.sum(scaled_grad * attended, axis=1))
        normed = (attended / radius[:, None] * gain).astype(jnp.bfloat16)
        out_delta = (scaled_grad / radius[:, None] - attended * (inner_sum / (FEAT * radius ** 3))[:, None]).astype(jnp.bfloat16)
        delta_block = out_delta.reshape(BLK, HEADS, DH)
        dprobs = masked_scores(delta_block, value_block, allowed)
        query_grad = jnp.einsum('hts,shd->thd', dprobs.astype(jnp.float32), key_block.astype(jnp.float32), precision=HIGHEST)
        query_grad = query_grad + jnp.einsum('thj,hij->thi', delta_block.astype(jnp.float32), state, precision=HIGHEST) * apply_in
        gather_in = (block_docs == doc_after).astype(jnp.float32)[:, None, None]
        keep = (doc_after == before).astype(jnp.float32)
        update = jnp.einsum('shi,shj->hij', key_block.astype(jnp.float32) * gather_in, value_block.astype(jnp.float32), precision=HIGHEST)
        return (keep * state + update, (normed, delta_block, query_grad.astype(jnp.bfloat16)))
    start_state = jnp.zeros((HEADS, DH, DH), jnp.float32)
    unused, (normed, delta_blocks, query_grad) = lax.scan(forward_step, start_state, (query_blocks, key_blocks, value_blocks, grad_blocks, doc_tok, doc_before[:-1], doc_before[1:]))

    def backward_step(carry, inputs):
        query_block, key_block, value_block, delta_block, block_docs, doc_start, doc_end = inputs
        allowed = causal & (block_docs[:, None] == block_docs[None, :])
        probs = masked_scores(query_block, key_block, allowed)
        dprobs = masked_scores(delta_block, value_block, allowed)
        apply_out = (block_docs == doc_end).astype(jnp.float32)[:, None, None]
        key_grad = jnp.einsum('hts,thd->shd', dprobs.astype(jnp.float32), query_block.astype(jnp.float32), precision=HIGHEST)
        key_grad = key_grad + jnp.einsum('shj,hij->shi', value_block.astype(jnp.float32), carry, precision=HIGHEST) * apply_out
        value_grad = jnp.einsum('hts,thd->shd', probs.astype(jnp.float32), delta_block.astype(jnp.float32), precision=HIGHEST)
        value_grad = value_grad + jnp.einsum('shi,hij->shj', key_block.astype(jnp.float32), carry, precision=HIGHEST) * apply_out
        gather_in = (block_docs == doc_start).astype(jnp.float32)[:, None, None]
        keep = (doc_start == doc_end).astype(jnp.float32)
        update = jnp.einsum('thi,thj->hij', query_block.astype(jnp.float32) * gather_in, delta_block.astype(jnp.float32), precision=HIGHEST)
        return (keep * carry + update, (key_grad.astype(jnp.bfloat16), value_grad.astype(jnp.bfloat16)))
    unused_back, (key_grad, value_grad) = lax.scan(backward_step, start_state, (query_blocks, key_blocks, value_blocks, delta_blocks, doc_tok, doc_at[:-1], doc_at[1:]), reverse=True)
    return (normed.reshape(TOKENS, FEAT), query_grad.reshape(TOKENS, FEAT), key_grad.reshape(TOKENS, FEAT), value_grad.reshape(TOKENS, FEAT))
```

```python
import functools

import jax
import jax.numpy as jnp
from jax import lax
from jax.experimental import pallas as pl
from jax.experimental.pallas import tpu as pltpu
from jax.sharding import PartitionSpec as P

DH = 128
BLK = 256
FEAT = 4096
EPSILON = 1e-06
TOK = 512
WIDE = 256
GROUP = 16
F32 = jnp.float32
BF16 = jnp.bfloat16


def dot(a, b, ca, cb):
    return lax.dot_general(a, b, (((ca,), (cb,)), ((), ())), preferred_element_type=F32)


def dot_state(a, s, cs):
    high = s.astype(BF16)
    low = (s - high.astype(F32)).astype(BF16)
    return dot(a, high, 1, cs) + dot(a, low, 1, cs)


def iota(shape, dim):
    return lax.broadcasted_iota(jnp.int32, shape, dim).astype(F32)


def doc_starts(lengths_ref):
    docs = lengths_ref.shape[1]
    lengths = jnp.broadcast_to(lengths_ref[...].astype(F32), (docs, docs))
    i, j = iota((docs, docs), 0), iota((docs, docs), 1)
    column = jnp.sum(jnp.where(j < i, lengths, 0.0), axis=1, keepdims=True)
    return jnp.sum(jnp.where(i == j, column, 0.0), axis=0, keepdims=True)


def start_of(starts, positions):
    return jnp.max(jnp.where(starts <= positions, starts, 0.0), axis=1, keepdims=True)


def first_token():
    return (lax.axis_index("ctx") * TOK).astype(F32)


def span(b):
    return slice(b * BLK, (b + 1) * BLK)


def head(h):
    return slice(h * DH, (h + 1) * DH)


def summary_kernel(lengths_ref, k_ref, v_ref, start_ref, part_ref, out_ref):
    starts = doc_starts(lengths_ref)
    rows = TOK + 8
    positions = first_token() + iota((rows, starts.shape[1]), 0)
    start_ref[...] = jnp.broadcast_to(start_of(starts, positions), (rows, DH))
    at = first_token() + iota((TOK, DH), 0)
    open_end = (at >= start_ref[TOK - 1 : TOK, :]).astype(F32)
    open_mid = (at[:BLK] >= start_ref[BLK - 1 : BLK, :]).astype(F32)
    for h in range(2):
        k = k_ref[:, head(h)].astype(F32)
        v = v_ref[:, head(h)]
        total = dot((k * open_end).astype(BF16), v, 0, 0)
        out_ref[h * 8 : (h + 1) * 8] = total.reshape(8, 16, DH)
        part_ref[head(h), :] = dot((k[:BLK] * open_mid).astype(BF16), v[:BLK], 0, 0)


def keeps(lengths_ref, reverse):
    starts = doc_starts(lengths_ref)
    group = lax.axis_index("ctx") // GROUP * GROUP
    left = (iota((GROUP, starts.shape[1]), 0) + group.astype(F32)) * TOK
    if reverse:
        return (start_of(starts, left + TOK) <= left[:, :1]).astype(F32)
    return (start_of(starts, left + (TOK - 1)) < left[:, :1]).astype(F32)


def total_kernel(reverse, lengths_ref, x_ref, out_ref):
    keep = keeps(lengths_ref, reverse)
    now = jnp.zeros(out_ref.shape, F32)
    for i in reversed(range(GROUP)) if reverse else range(GROUP):
        now = x_ref[i] + keep[i : i + 1, :] * now
    out_ref[...] = now


def prefix_kernel(reverse, lengths_ref, x_ref, before_ref, out_ref):
    keep = keeps(lengths_ref, reverse)
    now = before_ref[...]
    for i in reversed(range(GROUP)) if reverse else range(GROUP):
        out_ref[i] = now
        now = x_ref[i] + keep[i : i + 1, :] * now


def allowed(start_ref, b):
    start = start_ref[span(b), :] - (first_token() + b * BLK)
    start = jnp.concatenate([start, start], axis=1)
    t, s = iota((BLK, BLK), 0), iota((BLK, BLK), 1)
    return (s <= t) & (s >= start)


def within_kernel(start_ref, q_ref, k_ref, v_ref, probs_ref, within_ref):
    for b in range(2):
        mask = allowed(start_ref, b)
        for h in range(2):
            where = (span(b), head(h))
            scores = dot(q_ref[where], k_ref[where], 1, 1)
            probs = jnp.where(mask, scores, 0.0).astype(BF16)
            probs_ref[2 * b + h] = probs
            within_ref[where] = dot(probs, v_ref[where], 1, 0)


def entering(start_ref, state_ref, part_ref, b, h):
    state = state_ref[head(h), :]
    if b == 0:
        return state
    keep = (start_ref[BLK - 1 : BLK, :] < first_token()).astype(F32)
    return keep * state + part_ref[head(h), :]


def applies_fwd(start_ref, b):
    return (start_ref[span(b), :] < first_token() + b * BLK).astype(F32)


def attend_kernel(
    start_ref, q_ref, og_ref, gain_ref, within_ref, state_ref, part_ref, att_ref, sums_ref
):
    rows = []
    for b in range(2):
        apply = applies_fwd(start_ref, b)
        square, inner = 0.0, 0.0
        for h in range(2):
            where = (span(b), head(h))
            state = entering(start_ref, state_ref, part_ref, b, h)
            att = within_ref[where] + dot_state(q_ref[where], state, 0) * apply
            att_ref[where] = att
            scaled = og_ref[where].astype(F32) * gain_ref[:, head(h)]
            square = square + att * att
            inner = inner + scaled * att
        rows.append((square, inner))
    lines = []
    for which in range(2):
        for b in range(2):
            for c in range(2):
                piece = rows[b][which][c * DH : (c + 1) * DH]
                lines.append(jnp.sum(piece.T, axis=0, keepdims=True))
    sums = jnp.concatenate(lines, axis=0)
    for i in range(16):
        sums_ref[i] = sums


def tall(row):
    return jnp.concatenate(
        [jnp.broadcast_to(row[c : c + 1, :], (DH, DH)).T for c in range(4)], axis=0
    )


def delta_kernel(
    start_ref,
    q_ref,
    og_ref,
    gain_ref,
    att_ref,
    sums_ref,
    delta_ref,
    inverse_ref,
    part_ref,
    out_ref,
):
    sums = jnp.sum(sums_ref[...], axis=0)
    radius = jnp.sqrt(sums[:4] / FEAT + EPSILON)
    inverse = tall(1.0 / radius)
    factor = tall(sums[4:] / (FEAT * radius * radius * radius))
    inverse_ref[...] = inverse
    base = first_token()
    open_start = (start_ref[:TOK, :] <= base).astype(F32)
    open_mid = (start_ref[span(1), :] <= base + BLK).astype(F32)
    for h in range(2):
        scaled = og_ref[:, head(h)].astype(F32) * gain_ref[:, head(h)]
        delta = (scaled * inverse - att_ref[:, head(h)] * factor).astype(BF16)
        delta_ref[:, head(h)] = delta
        q = q_ref[:, head(h)].astype(F32)
        total = dot((q * open_start).astype(BF16), delta, 0, 0)
        out_ref[h * 8 : (h + 1) * 8] = total.reshape(8, 16, DH)
        part_ref[head(h), :] = dot((q[BLK:] * open_mid).astype(BF16), delta[BLK:], 0, 0)


def local_grads_kernel(
    start_ref,
    q_ref,
    k_ref,
    v_ref,
    gain_ref,
    att_ref,
    delta_ref,
    inverse_ref,
    probs_ref,
    state_ref,
    part_ref,
    normed_ref,
    qg_ref,
    kg_ref,
    vg_ref,
):
    for b in range(2):
        mask = allowed(start_ref, b)
        apply = applies_fwd(start_ref, b)
        for h in range(2):
            where = (span(b), head(h))
            normed_ref[where] = (
                att_ref[where] * inverse_ref[span(b), :] * gain_ref[:, head(h)]
            ).astype(BF16)
            delta = delta_ref[where]
            dprobs = jnp.where(mask, dot(delta, v_ref[where], 1, 1), 0.0).astype(BF16)
            state = entering(start_ref, state_ref, part_ref, b, h)
            qg_ref[where] = (
                dot(dprobs, k_ref[where], 1, 0) + dot_state(delta, state, 1) * apply
            ).astype(BF16)
            kg_ref[where] = dot(dprobs, q_ref[where], 0, 0)
            vg_ref[where] = dot(probs_ref[2 * b + h], delta, 0, 0)


def last_grads_kernel(
    start_ref, k_ref, v_ref, kg_in_ref, vg_in_ref, state_ref, part_ref, kg_ref, vg_ref
):
    base = first_token()
    keep = (start_ref[TOK : TOK + 1, :] <= base + BLK).astype(F32)
    for b in range(2):
        edge = (b + 1) * BLK
        at = base + b * BLK + iota((BLK, DH), 0)
        apply = (at >= start_ref[edge : edge + 1, :]).astype(F32)
        for h in range(2):
            where = (span(b), head(h))
            state = state_ref[head(h), :]
            if b == 0:
                state = keep * state + part_ref[head(h), :]
            kg = kg_in_ref[where] + dot_state(v_ref[where], state, 1) * apply
            vg = vg_in_ref[where] + dot_state(k_ref[where], state, 0) * apply
            kg_ref[where] = kg.astype(BF16)
            vg_ref[where] = vg.astype(BF16)


def call(kernel, outs, *args, flops=0, name=None):
    shapes = [jax.ShapeDtypeStruct(s, d) for s, d in outs]
    moved = sum(a.size * a.dtype.itemsize for a in args)
    moved += sum(s.size * s.dtype.itemsize for s in shapes)
    return pl.pallas_call(
        kernel,
        out_shape=shapes,
        compiler_params=pltpu.CompilerParams(vmem_limit_bytes=40 << 20),
        cost_estimate=pl.CostEstimate(flops=flops, bytes_accessed=moved, transcendentals=0),
        name=name,
    )(*args)


def carried(lengths, summary, reverse):
    step = -GROUP if reverse else GROUP
    count = lax.axis_size("ctx")
    groups = [list(range(g, g + GROUP)) for g in range(0, count, GROUP)]
    pairs = [(i, i + step) for i in range(count) if 0 <= i + step < count]
    piece = (GROUP, DH)
    whole = (GROUP, GROUP, DH)
    x = lax.all_to_all(summary, "ctx", 0, 0, axis_index_groups=groups)
    (total,) = call(functools.partial(total_kernel, reverse), [(piece, F32)], lengths, x)
    before = lax.ppermute(total, "ctx", pairs)
    (y,) = call(functools.partial(prefix_kernel, reverse), [(whole, F32)], lengths, x, before)
    y = lax.all_to_all(y, "ctx", 0, 0, axis_index_groups=groups)
    return y.reshape(2 * DH, DH)


def body(q, k, v, og, gain, lengths):
    lengths = lengths.reshape(1, -1)
    gain = gain.reshape(1, -1)
    tokens = (TOK, WIDE)
    states = (2 * DH, DH)
    pieces = (GROUP, GROUP, DH)
    start, part, summary = call(
        summary_kernel,
        [((TOK + 8, DH), F32), (states, F32), (pieces, F32)],
        lengths,
        k,
        v,
        flops=1 << 26,
        name="summary",
    )
    state = carried(lengths, summary, False)
    probs, within = call(
        within_kernel,
        [((4, BLK, BLK), BF16), (tokens, F32)],
        start,
        q,
        k,
        v,
        flops=1 << 28,
        name="within",
    )
    att, sums = call(
        attend_kernel,
        [(tokens, F32), ((16, 8, DH), F32)],
        start,
        q,
        og,
        gain,
        within,
        state,
        part,
        flops=1 << 27,
        name="attend",
    )
    sums = lax.all_to_all(sums, "head", 0, 0)
    delta, inverse, part_back, summary = call(
        delta_kernel,
        [(tokens, BF16), ((TOK, DH), F32), (states, F32), (pieces, F32)],
        start,
        q,
        og,
        gain,
        att,
        sums,
        flops=1 << 26,
        name="delta",
    )
    state_back = carried(lengths, summary, True)
    normed, qg, kg, vg = call(
        local_grads_kernel,
        [(tokens, BF16), (tokens, BF16), (tokens, F32), (tokens, F32)],
        start,
        q,
        k,
        v,
        gain,
        att,
        delta,
        inverse,
        probs,
        state,
        part,
        flops=1 << 29,
        name="local_grads",
    )
    kg, vg = call(
        last_grads_kernel,
        [(tokens, BF16), (tokens, BF16)],
        start,
        k,
        v,
        kg,
        vg,
        state_back,
        part_back,
        flops=1 << 28,
        name="last_grads",
    )
    return normed, qg, kg, vg


def solution(mesh):
    both = P("ctx", "head")
    return jax.shard_map(
        body,
        mesh=mesh,
        in_specs=(both, both, both, both, P("head"), P()),
        out_specs=(both, both, both, both),
        check_vma=False,
    )
```

```python
import functools

import jax
import jax.numpy as jnp
from jax import lax
from jax.experimental import pallas as pl
from jax.experimental.pallas import tpu as pltpu
from jax.sharding import PartitionSpec as P

DH = 128
BLK = 256
FEAT = 4096
EPSILON = 1e-06
TOK = 512
WIDE = 256
CHUNK = 256
GROUP = 16
F32 = jnp.float32
BF16 = jnp.bfloat16


def dot(a, b, ca, cb):
    return lax.dot_general(a, b, (((ca,), (cb,)), ((), ())), preferred_element_type=F32)


def dot_state(a, s, cs):
    high = s.astype(BF16)
    low = (s - high.astype(F32)).astype(BF16)
    return dot(a, high, 1, cs) + dot(a, low, 1, cs)


def iota(shape, dim):
    return lax.broadcasted_iota(jnp.int32, shape, dim).astype(F32)


def doc_starts(lengths_ref):
    docs = lengths_ref.shape[1]
    lengths = jnp.broadcast_to(lengths_ref[...].astype(F32), (docs, docs))
    i, j = iota((docs, docs), 0), iota((docs, docs), 1)
    column = jnp.sum(jnp.where(j < i, lengths, 0.0), axis=1, keepdims=True)
    return jnp.sum(jnp.where(i == j, column, 0.0), axis=0, keepdims=True)


def start_of(starts, positions):
    return jnp.max(jnp.where(starts <= positions, starts, 0.0), axis=1, keepdims=True)


def first_token():
    return (lax.axis_index("ctx") * TOK).astype(F32)


def span(b):
    return slice(b * BLK, (b + 1) * BLK)


def head(h):
    return slice(h * DH, (h + 1) * DH)


def summary_kernel(lengths_hbm, k_hbm, v_hbm, out_ref, lengths, k_in, v_in, sems):
    parts = range(0, TOK, CHUNK)
    first = pltpu.make_async_copy(lengths_hbm, lengths, sems.at[0])
    first.start()
    copies = []
    for n, at in enumerate(parts):
        rows = slice(at, at + CHUNK)
        for m, (hbm, ref) in enumerate(((k_hbm, k_in), (v_hbm, v_in))):
            copy = pltpu.make_async_copy(hbm.at[rows], ref.at[rows], sems.at[1 + 2 * n + m])
            copy.start()
            copies.append(copy)
    first.wait()
    starts = doc_starts(lengths)
    last = jnp.broadcast_to(first_token() + (TOK - 1), (8, starts.shape[1]))
    start = start_of(starts, last)[:1] - first_token()
    totals = [0.0, 0.0]
    for n, at in enumerate(parts):
        copies[2 * n].wait()
        copies[2 * n + 1].wait()
        rows = slice(at, at + CHUNK)
        open_end = (iota((CHUNK, DH), 0) + at >= start).astype(F32)
        for h in range(2):
            k = k_in[rows, head(h)].astype(F32)
            totals[h] = totals[h] + dot((k * open_end).astype(BF16), v_in[rows, head(h)], 0, 0)
    for h in range(2):
        out_ref[h * 8 : (h + 1) * 8] = totals[h].reshape(8, 16, DH)


def keeps(starts, reverse):
    group = lax.axis_index("ctx") // GROUP * GROUP
    left = (iota((GROUP, starts.shape[1]), 0) + group.astype(F32)) * TOK
    if reverse:
        return (start_of(starts, left + TOK) <= left[:, :1]).astype(F32)
    return (start_of(starts, left + (TOK - 1)) < left[:, :1]).astype(F32)


def order(reverse):
    return reversed(range(GROUP)) if reverse else range(GROUP)


def total_kernel(reverse, lengths_ref, x_ref, out_ref):
    keep = keeps(doc_starts(lengths_ref), reverse)
    now = jnp.zeros(out_ref.shape, F32)
    for i in order(reverse):
        now = x_ref[i] + keep[i : i + 1, :] * now
    out_ref[...] = now


def group_prefix(reverse, starts, x_ref, prefix_ref, open_ref):
    keep = keeps(starts, reverse)
    now = jnp.zeros(x_ref.shape[1:], F32)
    still = jnp.ones((1, DH), F32)
    for i in order(reverse):
        prefix_ref[i] = now
        open_ref[i : i + 1, :] = still
        now = x_ref[i] + keep[i : i + 1, :] * now
        still = keep[i : i + 1, :] * still


def join_kernel(prefix_ref, open_ref, before_ref, out_ref):
    before = before_ref[...]
    for i in range(GROUP):
        out_ref[i] = prefix_ref[i] + open_ref[i : i + 1, :] * before


def allowed(start_ref, b):
    start = start_ref[span(b), :] - (first_token() + b * BLK)
    start = jnp.concatenate([start, start], axis=1)
    t, s = iota((BLK, BLK), 0), iota((BLK, BLK), 1)
    return (s <= t) & (s >= start)


def within_kernel(
    lengths_ref,
    x_ref,
    q_ref,
    k_ref,
    v_ref,
    og_ref,
    gain_ref,
    prefix_ref,
    open_ref,
    start_ref,
    probs_ref,
    within_ref,
    scaled_ref,
    part_ref,
):
    starts = doc_starts(lengths_ref)
    group_prefix(False, starts, x_ref, prefix_ref, open_ref)
    positions = first_token() + iota((TOK + 8, starts.shape[1]), 0)
    start_ref[...] = jnp.broadcast_to(start_of(starts, positions), start_ref.shape)
    at = first_token() + iota((BLK, DH), 0)
    open_mid = (at >= start_ref[BLK - 1 : BLK, :]).astype(F32)
    for h in range(2):
        k = k_ref[:BLK, head(h)].astype(F32)
        part_ref[head(h), :] = dot((k * open_mid).astype(BF16), v_ref[:BLK, head(h)], 0, 0)
    for b in range(2):
        mask = allowed(start_ref, b)
        for h in range(2):
            where = (span(b), head(h))
            scores = dot(q_ref[where], k_ref[where], 1, 1)
            probs = jnp.where(mask, scores, 0.0).astype(BF16)
            probs_ref[2 * b + h] = probs
            within_ref[where] = dot(probs, v_ref[where], 1, 0)
            scaled_ref[where] = og_ref[where].astype(F32) * gain_ref[:, head(h)]


def entering(start_ref, state_ref, part_ref, b, h):
    state = state_ref[head(h), :]
    if b == 0:
        return state
    keep = (start_ref[BLK - 1 : BLK, :] < first_token()).astype(F32)
    return keep * state + part_ref[head(h), :]


def applies_fwd(start_ref, b):
    return (start_ref[span(b), :] < first_token() + b * BLK).astype(F32)


def attend_kernel(
    start_ref, q_ref, scaled_ref, within_ref, state_ref, part_ref, att_ref, sums_ref
):
    rows = []
    for b in range(2):
        apply = applies_fwd(start_ref, b)
        square, inner = 0.0, 0.0
        for h in range(2):
            where = (span(b), head(h))
            state = entering(start_ref, state_ref, part_ref, b, h)
            att = within_ref[where] + dot_state(q_ref[where], state, 0) * apply
            att_ref[where] = att
            scaled = scaled_ref[where]
            square = square + att * att
            inner = inner + scaled * att
        rows.append((square, inner))
    lines = []
    for which in range(2):
        for b in range(2):
            for c in range(2):
                piece = rows[b][which][c * DH : (c + 1) * DH]
                lines.append(jnp.sum(piece.T, axis=0, keepdims=True))
    sums = jnp.concatenate(lines, axis=0)
    for i in range(16):
        sums_ref[i] = sums


def tall(row):
    return jnp.concatenate(
        [jnp.broadcast_to(row[c : c + 1, :], (DH, DH)).T for c in range(4)], axis=0
    )


def delta_kernel(start_ref, q_ref, scaled_ref, att_ref, sums_ref, delta_ref, out_ref):
    sums = jnp.sum(sums_ref[...], axis=0)
    radius = jnp.sqrt(sums[:4] / FEAT + EPSILON)
    inverse = tall(1.0 / radius)
    factor = tall(sums[4:] / (FEAT * radius * radius * radius))
    open_start = (start_ref[:TOK, :] <= first_token()).astype(F32)
    for h in range(2):
        delta = scaled_ref[:, head(h)] * inverse - att_ref[:, head(h)] * factor
        delta = delta.astype(BF16)
        delta_ref[:, head(h)] = delta
        q = q_ref[:, head(h)].astype(F32)
        total = dot((q * open_start).astype(BF16), delta, 0, 0)
        out_ref[h * 8 : (h + 1) * 8] = total.reshape(8, 16, DH)


def local_grads_kernel(
    lengths_ref,
    start_ref,
    x_ref,
    q_ref,
    k_ref,
    v_ref,
    gain_ref,
    att_ref,
    delta_ref,
    sums_ref,
    probs_ref,
    state_ref,
    part_ref,
    prefix_ref,
    open_ref,
    normed_ref,
    qg_ref,
    kg_ref,
    vg_ref,
    back_ref,
):
    group_prefix(True, doc_starts(lengths_ref), x_ref, prefix_ref, open_ref)
    sums = jnp.sum(sums_ref[...], axis=0)
    inverse = tall(1.0 / jnp.sqrt(sums[:4] / FEAT + EPSILON))
    open_mid = (start_ref[span(1), :] <= first_token() + BLK).astype(F32)
    for h in range(2):
        q = q_ref[BLK:, head(h)].astype(F32)
        back_ref[head(h), :] = dot((q * open_mid).astype(BF16), delta_ref[BLK:, head(h)], 0, 0)
    for b in range(2):
        mask = allowed(start_ref, b)
        apply = applies_fwd(start_ref, b)
        for h in range(2):
            where = (span(b), head(h))
            normed_ref[where] = (att_ref[where] * inverse[span(b)] * gain_ref[:, head(h)]).astype(
                BF16
            )
            delta = delta_ref[where]
            dprobs = jnp.where(mask, dot(delta, v_ref[where], 1, 1), 0.0).astype(BF16)
            state = entering(start_ref, state_ref, part_ref, b, h)
            qg_ref[where] = (
                dot(dprobs, k_ref[where], 1, 0) + dot_state(delta, state, 1) * apply
            ).astype(BF16)
            kg_ref[where] = dot(dprobs, q_ref[where], 0, 0)
            vg_ref[where] = dot(probs_ref[2 * b + h], delta, 0, 0)


def last_grads_kernel(
    start_ref,
    k_ref,
    v_ref,
    kg_in_ref,
    vg_in_ref,
    state_ref,
    part_ref,
    kg_hbm,
    vg_hbm,
    kg_ref,
    vg_ref,
    sems,
):
    base = first_token()
    keep = (start_ref[TOK : TOK + 1, :] <= base + BLK).astype(F32)
    copies = []
    for b in range(2):
        edge = (b + 1) * BLK
        at = base + b * BLK + iota((BLK, DH), 0)
        apply = (at >= start_ref[edge : edge + 1, :]).astype(F32)
        for h in range(2):
            where = (span(b), head(h))
            state = state_ref[head(h), :]
            if b == 0:
                state = keep * state + part_ref[head(h), :]
            kg = kg_in_ref[where] + dot_state(v_ref[where], state, 1) * apply
            vg = vg_in_ref[where] + dot_state(k_ref[where], state, 0) * apply
            kg_ref[where] = kg.astype(BF16)
            vg_ref[where] = vg.astype(BF16)
        for i, (ref, hbm) in enumerate(((kg_ref, kg_hbm), (vg_ref, vg_hbm))):
            copy = pltpu.make_async_copy(ref.at[span(b)], hbm.at[span(b)], sems.at[b, i])
            copy.start()
            copies.append(copy)
    for copy in copies:
        copy.wait()


def call(kernel, outs, *args, flops=0, name=None, grant=24, bound=True, **rest):
    shapes = [jax.ShapeDtypeStruct(s, d) for s, d in outs]
    moved = sum(a.size * a.dtype.itemsize for a in args)
    moved += sum(s.size * s.dtype.itemsize for s in shapes)
    moved = moved if bound else 0
    return pl.pallas_call(
        kernel,
        out_shape=shapes,
        compiler_params=pltpu.CompilerParams(vmem_limit_bytes=grant << 20),
        cost_estimate=pl.CostEstimate(flops=flops, bytes_accessed=moved, transcendentals=0),
        name=name,
        **rest,
    )(*args)


HBM = pl.BlockSpec(memory_space=pltpu.HBM)
VMEM = pl.BlockSpec(memory_space=pltpu.VMEM)
TOKENS = (TOK, WIDE)
STATES = (2 * DH, DH)
PIECE = (GROUP, DH)
PIECES = (GROUP, GROUP, DH)


def swap(x):
    count = lax.axis_size("ctx")
    groups = [list(range(g, g + GROUP)) for g in range(0, count, GROUP)]
    return lax.all_to_all(x, "ctx", 0, 0, axis_index_groups=groups)


def total_before(lengths, x, reverse):
    step = -GROUP if reverse else GROUP
    count = lax.axis_size("ctx")
    pairs = [(i, i + step) for i in range(count) if 0 <= i + step < count]
    kernel = functools.partial(total_kernel, reverse)
    (total,) = call(kernel, [(PIECE, F32)], lengths, x, name="total")
    return lax.ppermute(total, "ctx", pairs)


def joined(prefix, still, before):
    (y,) = call(join_kernel, [(PIECES, F32)], prefix, still, before, name="join")
    return swap(y).reshape(STATES)


def body(q, k, v, og, gain, lengths):
    lengths = lengths.reshape(1, -1)
    gain = gain.reshape(1, -1)
    docs = lengths.shape
    (summary,) = call(
        summary_kernel,
        [(PIECES, F32)],
        lengths,
        k,
        v,
        flops=1 << 26,
        name="summary",
        grant=60,
        in_specs=[HBM] * 3,
        scratch_shapes=[
            pltpu.VMEM(docs, jnp.int32),
            pltpu.VMEM(TOKENS, BF16),
            pltpu.VMEM(TOKENS, BF16),
            pltpu.SemaphoreType.DMA((1 + 2 * (TOK // CHUNK),)),
        ],
    )
    x = swap(summary)
    before = total_before(lengths, x, False)
    prefix, still, start, probs, within, scaled, part = call(
        within_kernel,
        [
            (PIECES, F32),
            (PIECE, F32),
            ((TOK + 8, DH), F32),
            ((4, BLK, BLK), BF16),
            (TOKENS, F32),
            (TOKENS, F32),
            (STATES, F32),
        ],
        lengths,
        x,
        q,
        k,
        v,
        og,
        gain,
        flops=1 << 28,
        name="within",
    )
    state = joined(prefix, still, before)
    att, sums = call(
        attend_kernel,
        [(TOKENS, F32), ((16, 8, DH), F32)],
        start,
        q,
        scaled,
        within,
        state,
        part,
        flops=1 << 27,
        name="attend",
    )
    sums = lax.all_to_all(sums, "head", 0, 0)
    delta, summary = call(
        delta_kernel,
        [(TOKENS, BF16), (PIECES, F32)],
        start,
        q,
        scaled,
        att,
        sums,
        flops=1 << 26,
        name="delta",
    )
    x = swap(summary)
    before = total_before(lengths, x, True)
    prefix, still, normed, qg, kg, vg, part_back = call(
        local_grads_kernel,
        [
            (PIECES, F32),
            (PIECE, F32),
            (TOKENS, BF16),
            (TOKENS, BF16),
            (TOKENS, F32),
            (TOKENS, F32),
            (STATES, F32),
        ],
        lengths,
        start,
        x,
        q,
        k,
        v,
        gain,
        att,
        delta,
        sums,
        probs,
        state,
        part,
        flops=1 << 29,
        name="local_grads",
    )
    state_back = joined(prefix, still, before)
    kg, vg = call(
        last_grads_kernel,
        [(TOKENS, BF16), (TOKENS, BF16)],
        start,
        k,
        v,
        kg,
        vg,
        state_back,
        part_back,
        flops=1 << 28,
        name="last_grads",
        in_specs=[VMEM] * 7,
        out_specs=[HBM] * 2,
        scratch_shapes=[
            pltpu.VMEM(TOKENS, BF16),
            pltpu.VMEM(TOKENS, BF16),
            pltpu.SemaphoreType.DMA((2, 2)),
        ],
    )
    return normed, qg, kg, vg


def solution(mesh):
    both = P("ctx", "head")
    return jax.shard_map(
        body,
        mesh=mesh,
        in_specs=(both, both, both, both, P("head"), P()),
        out_specs=(both, both, both, both),
        check_vma=False,
    )
```

```python
import functools

import jax
import jax.numpy as jnp
from jax import lax
from jax.experimental import pallas as pl
from jax.experimental.pallas import tpu as pltpu
from jax.sharding import PartitionSpec as P

DH = 128
BLK = 256
FEAT = 4096
EPSILON = 1e-06
TOK = 512
WIDE = 256
CHUNK = 256
GROUP = 16
F32 = jnp.float32
BF16 = jnp.bfloat16


def dot(a, b, ca, cb):
    return lax.dot_general(a, b, (((ca,), (cb,)), ((), ())), preferred_element_type=F32)


def iota(shape, dim):
    return lax.broadcasted_iota(jnp.int32, shape, dim).astype(F32)


def doc_starts(lengths_ref):
    docs = lengths_ref.shape[1]
    lengths = jnp.broadcast_to(lengths_ref[...].astype(F32), (docs, docs))
    i, j = iota((docs, docs), 0), iota((docs, docs), 1)
    column = jnp.sum(jnp.where(j < i, lengths, 0.0), axis=1, keepdims=True)
    return jnp.sum(jnp.where(i == j, column, 0.0), axis=0, keepdims=True)


def start_of(starts, positions):
    return jnp.max(jnp.where(starts <= positions, starts, 0.0), axis=1, keepdims=True)


def first_token():
    return (lax.axis_index("ctx") * TOK).astype(F32)


def span(b):
    return slice(b * BLK, (b + 1) * BLK)


def head(h):
    return slice(h * DH, (h + 1) * DH)


def diagonal(total):
    return [total[head(h), head(h)].reshape(8, 16, DH) for h in range(2)]


def summary_kernel(lengths_hbm, k_hbm, v_hbm, lengths_ref, k_ref, v_ref, out_ref, sems):
    parts = range(0, TOK, CHUNK)
    first = pltpu.make_async_copy(lengths_hbm, lengths_ref, sems.at[0])
    first.start()
    copies = []
    for n, at in enumerate(parts):
        rows = slice(at, at + CHUNK)
        for m, (hbm, ref) in enumerate(((k_hbm, k_ref), (v_hbm, v_ref))):
            copy = pltpu.make_async_copy(hbm.at[rows], ref.at[rows], sems.at[1 + 2 * n + m])
            copy.start()
            copies.append(copy)
    first.wait()
    starts = doc_starts(lengths_ref)
    last = jnp.broadcast_to(first_token() + (TOK - 1), (8, starts.shape[1]))
    start = start_of(starts, last)[:1] - first_token()
    total = 0.0
    for n, at in enumerate(parts):
        copies[2 * n].wait()
        copies[2 * n + 1].wait()
        rows = slice(at, at + CHUNK)
        open_end = (iota((CHUNK, WIDE), 0) + at >= start).astype(F32)
        k = (k_ref[rows].astype(F32) * open_end).astype(BF16)
        total = total + dot(k, v_ref[rows], 0, 0)
    for h, piece in enumerate(diagonal(total)):
        out_ref[h * 8 : (h + 1) * 8] = piece


def keeps(starts, reverse):
    group = lax.axis_index("ctx") // GROUP * GROUP
    left = (iota((GROUP, starts.shape[1]), 0) + group.astype(F32)) * TOK
    if reverse:
        return (start_of(starts, left + TOK) <= left[:, :1]).astype(F32)
    return (start_of(starts, left + (TOK - 1)) < left[:, :1]).astype(F32)


def order(reverse):
    return reversed(range(GROUP)) if reverse else range(GROUP)


def total_kernel(reverse, lengths_ref, x_ref, out_ref):
    keep = keeps(doc_starts(lengths_ref), reverse)
    now = jnp.zeros(out_ref.shape, F32)
    for i in order(reverse):
        now = x_ref[i] + keep[i : i + 1, :] * now
    out_ref[...] = now


def group_prefix(reverse, starts, x_ref, prefix_ref, open_ref):
    keep = keeps(starts, reverse)
    now = jnp.zeros(x_ref.shape[1:], F32)
    still = jnp.ones((1, DH), F32)
    for i in order(reverse):
        prefix_ref[i] = now
        open_ref[i : i + 1, :] = still
        now = x_ref[i] + keep[i : i + 1, :] * now
        still = keep[i : i + 1, :] * still


def join_kernel(prefix_ref, open_ref, before_ref, out_ref):
    before = before_ref[...]
    for i in range(GROUP):
        out_ref[i] = prefix_ref[i] + open_ref[i : i + 1, :] * before


def allowed(start_ref, b):
    start = start_ref[span(b), :] - (first_token() + b * BLK)
    start = jnp.concatenate([start, start], axis=1)
    t, s = iota((BLK, BLK), 0), iota((BLK, BLK), 1)
    return (s <= t) & (s >= start)


def within_kernel(
    lengths_ref,
    x_ref,
    q_ref,
    k_ref,
    v_ref,
    og_ref,
    gain_ref,
    prefix_ref,
    open_ref,
    start_ref,
    probs_ref,
    within_ref,
    scaled_ref,
    part_ref,
):
    starts = doc_starts(lengths_ref)
    group_prefix(False, starts, x_ref, prefix_ref, open_ref)
    positions = first_token() + iota((TOK + 8, starts.shape[1]), 0)
    start_ref[...] = jnp.broadcast_to(start_of(starts, positions), start_ref.shape)
    at = first_token() + iota((BLK, DH), 0)
    open_mid = (at >= start_ref[BLK - 1 : BLK, :]).astype(F32)
    for h in range(2):
        k = k_ref[:BLK, head(h)].astype(F32)
        part_ref[head(h), :] = dot((k * open_mid).astype(BF16), v_ref[:BLK, head(h)], 0, 0)
    for b in range(2):
        mask = allowed(start_ref, b)
        for h in range(2):
            where = (span(b), head(h))
            scores = dot(q_ref[where], k_ref[where], 1, 1)
            probs = jnp.where(mask, scores, 0.0).astype(BF16)
            probs_ref[2 * b + h] = probs
            within_ref[where] = dot(probs, v_ref[where], 1, 0)
            scaled_ref[where] = og_ref[where].astype(F32) * gain_ref[:, head(h)]


def both_heads(state):
    zero = jnp.zeros((DH, DH), F32)
    whole = jnp.concatenate(
        [
            jnp.concatenate([state[head(0)], zero], axis=1),
            jnp.concatenate([zero, state[head(1)]], axis=1),
        ],
        axis=0,
    )
    high = whole.astype(BF16)
    return high, (whole - high.astype(F32)).astype(BF16)


def dot_state(a, state, cs):
    return dot(a, state[0], 1, cs) + dot(a, state[1], 1, cs)


def entering(start_ref, state_ref, part_ref, b):
    state = state_ref[...]
    if b == 1:
        keep = (start_ref[BLK - 1 : BLK, :] < first_token()).astype(F32)
        state = keep * state + part_ref[...]
    return both_heads(state)


def twice(x):
    return jnp.concatenate([x, x], axis=1)


def applies_fwd(start_ref, b):
    return (start_ref[span(b), :] < first_token() + b * BLK).astype(F32)


def attend_kernel(
    start_ref, q_ref, scaled_ref, within_ref, state_ref, part_ref, att_ref, sums_ref
):
    rows = []
    for b in range(2):
        state = entering(start_ref, state_ref, part_ref, b)
        across = dot_state(q_ref[span(b)], state, 0)
        att = within_ref[span(b)] + across * twice(applies_fwd(start_ref, b))
        att_ref[span(b)] = att
        square, inner = att * att, scaled_ref[span(b)] * att
        rows.append((square[:, :DH] + square[:, DH:], inner[:, :DH] + inner[:, DH:]))
    lines = []
    for which in range(2):
        for b in range(2):
            for c in range(2):
                piece = rows[b][which][c * DH : (c + 1) * DH]
                lines.append(jnp.sum(piece.T, axis=0, keepdims=True))
    sums = jnp.concatenate(lines, axis=0)
    for i in range(16):
        sums_ref[i] = sums


def tall(row):
    return jnp.concatenate(
        [jnp.broadcast_to(row[c : c + 1, :], (DH, DH)).T for c in range(4)], axis=0
    )


def delta_kernel(start_ref, q_ref, scaled_ref, att_ref, sums_ref, delta_ref, out_ref):
    sums = jnp.sum(sums_ref[...], axis=0)
    radius = jnp.sqrt(sums[:4] / FEAT + EPSILON)
    inverse = twice(tall(1.0 / radius))
    factor = twice(tall(sums[4:] / (FEAT * radius * radius * radius)))
    open_start = twice((start_ref[:TOK, :] <= first_token()).astype(F32))
    delta = (scaled_ref[...] * inverse - att_ref[...] * factor).astype(BF16)
    delta_ref[...] = delta
    q = (q_ref[...].astype(F32) * open_start).astype(BF16)
    for h, piece in enumerate(diagonal(dot(q, delta, 0, 0))):
        out_ref[h * 8 : (h + 1) * 8] = piece


def local_grads_kernel(
    lengths_ref,
    start_ref,
    x_ref,
    q_ref,
    k_ref,
    v_ref,
    gain_ref,
    att_ref,
    delta_ref,
    sums_ref,
    probs_ref,
    state_ref,
    part_ref,
    prefix_ref,
    open_ref,
    normed_ref,
    qg_ref,
    kg_ref,
    vg_ref,
    back_ref,
):
    group_prefix(True, doc_starts(lengths_ref), x_ref, prefix_ref, open_ref)
    sums = jnp.sum(sums_ref[...], axis=0)
    inverse = tall(1.0 / jnp.sqrt(sums[:4] / FEAT + EPSILON))
    open_mid = (start_ref[span(1), :] <= first_token() + BLK).astype(F32)
    for h in range(2):
        q = q_ref[BLK:, head(h)].astype(F32)
        back_ref[head(h), :] = dot((q * open_mid).astype(BF16), delta_ref[BLK:, head(h)], 0, 0)
    for b in range(2):
        mask = allowed(start_ref, b)
        apply = twice(applies_fwd(start_ref, b))
        state = entering(start_ref, state_ref, part_ref, b)
        across = dot_state(delta_ref[span(b)], state, 1) * apply
        for h in range(2):
            where = (span(b), head(h))
            normed_ref[where] = (att_ref[where] * inverse[span(b)] * gain_ref[:, head(h)]).astype(
                BF16
            )
            delta = delta_ref[where]
            dprobs = jnp.where(mask, dot(delta, v_ref[where], 1, 1), 0.0).astype(BF16)
            qg_ref[where] = (dot(dprobs, k_ref[where], 1, 0) + across[:, head(h)]).astype(BF16)
            kg_ref[where] = dot(dprobs, q_ref[where], 0, 0)
            vg_ref[where] = dot(probs_ref[2 * b + h], delta, 0, 0)


def last_grads_kernel(
    start_ref,
    k_ref,
    v_ref,
    kg_in_ref,
    vg_in_ref,
    state_ref,
    part_ref,
    kg_hbm,
    vg_hbm,
    kg_ref,
    vg_ref,
    sems,
):
    base = first_token()
    keep = (start_ref[TOK : TOK + 1, :] <= base + BLK).astype(F32)
    copies = []
    for b in range(2):
        edge = (b + 1) * BLK
        at = base + b * BLK + iota((BLK, DH), 0)
        apply = twice((at >= start_ref[edge : edge + 1, :]).astype(F32))
        state = state_ref[...]
        if b == 0:
            state = keep * state + part_ref[...]
        state = both_heads(state)
        kg = kg_in_ref[span(b)] + dot_state(v_ref[span(b)], state, 1) * apply
        kg_ref[span(b)] = kg.astype(BF16)
        vg = vg_in_ref[span(b)] + dot_state(k_ref[span(b)], state, 0) * apply
        vg_ref[span(b)] = vg.astype(BF16)
        for i, (ref, hbm) in enumerate(((kg_ref, kg_hbm), (vg_ref, vg_hbm))):
            copy = pltpu.make_async_copy(ref.at[span(b)], hbm.at[span(b)], sems.at[b, i])
            copy.start()
            copies.append(copy)
    for copy in copies:
        copy.wait()


def call(kernel, outs, *args, flops=0, name=None, grant=24, bound=True, **rest):
    shapes = [jax.ShapeDtypeStruct(s, d) for s, d in outs]
    moved = sum(a.size * a.dtype.itemsize for a in args)
    moved += sum(s.size * s.dtype.itemsize for s in shapes)
    moved = moved if bound else 0
    return pl.pallas_call(
        kernel,
        out_shape=shapes,
        compiler_params=pltpu.CompilerParams(vmem_limit_bytes=grant << 20),
        cost_estimate=pl.CostEstimate(flops=flops, bytes_accessed=moved, transcendentals=0),
        name=name,
        **rest,
    )(*args)


HBM = pl.BlockSpec(memory_space=pltpu.HBM)
VMEM = pl.BlockSpec(memory_space=pltpu.VMEM)
TOKENS = (TOK, WIDE)
STATES = (2 * DH, DH)
PIECE = (GROUP, DH)
PIECES = (GROUP, GROUP, DH)


def swap(x):
    count = lax.axis_size("ctx")
    groups = [list(range(g, g + GROUP)) for g in range(0, count, GROUP)]
    return lax.all_to_all(x, "ctx", 0, 0, axis_index_groups=groups)


def total_before(lengths, x, reverse):
    step = -GROUP if reverse else GROUP
    count = lax.axis_size("ctx")
    pairs = [(i, i + step) for i in range(count) if 0 <= i + step < count]
    kernel = functools.partial(total_kernel, reverse)
    (total,) = call(kernel, [(PIECE, F32)], lengths, x, name="total")
    return lax.ppermute(total, "ctx", pairs)


def joined(prefix, still, before):
    (y,) = call(join_kernel, [(PIECES, F32)], prefix, still, before, name="join")
    return swap(y).reshape(STATES)


def body(q, k, v, og, gain, lengths):
    lengths = lengths.reshape(1, -1)
    gain = gain.reshape(1, -1)
    docs = lengths.shape
    lengths, k, v, summary = call(
        summary_kernel,
        [(docs, jnp.int32), (TOKENS, BF16), (TOKENS, BF16), (PIECES, F32)],
        *(pltpu.with_memory_space_constraint(a, pltpu.HBM) for a in (lengths, k, v)),
        flops=1 << 26,
        name="summary",
        in_specs=[HBM] * 3,
        scratch_shapes=[pltpu.SemaphoreType.DMA((1 + 2 * (TOK // CHUNK),))],
    )
    q, og, summary = lax.optimization_barrier((q, og, summary))
    x = swap(summary)
    before = total_before(lengths, x, False)
    prefix, still, start, probs, within, scaled, part = call(
        within_kernel,
        [
            (PIECES, F32),
            (PIECE, F32),
            ((TOK + 8, DH), F32),
            ((4, BLK, BLK), BF16),
            (TOKENS, F32),
            (TOKENS, F32),
            (STATES, F32),
        ],
        lengths,
        x,
        q,
        k,
        v,
        og,
        gain,
        flops=1 << 28,
        name="within",
    )
    state = joined(prefix, still, before)
    att, sums = call(
        attend_kernel,
        [(TOKENS, F32), ((16, 8, DH), F32)],
        start,
        q,
        scaled,
        within,
        state,
        part,
        flops=1 << 27,
        name="attend",
    )
    sums = lax.all_to_all(sums, "head", 0, 0)
    delta, summary = call(
        delta_kernel,
        [(TOKENS, BF16), (PIECES, F32)],
        start,
        q,
        scaled,
        att,
        sums,
        flops=1 << 26,
        name="delta",
    )
    x = swap(summary)
    before = total_before(lengths, x, True)
    prefix, still, normed, qg, kg, vg, part_back = call(
        local_grads_kernel,
        [
            (PIECES, F32),
            (PIECE, F32),
            (TOKENS, BF16),
            (TOKENS, BF16),
            (TOKENS, F32),
            (TOKENS, F32),
            (STATES, F32),
        ],
        lengths,
        start,
        x,
        q,
        k,
        v,
        gain,
        att,
        delta,
        sums,
        probs,
        state,
        part,
        flops=1 << 29,
        name="local_grads",
    )
    state_back = joined(prefix, still, before)
    kg, vg = call(
        last_grads_kernel,
        [(TOKENS, BF16), (TOKENS, BF16)],
        start,
        k,
        v,
        kg,
        vg,
        state_back,
        part_back,
        flops=1 << 28,
        name="last_grads",
        in_specs=[VMEM] * 7,
        out_specs=[HBM] * 2,
        scratch_shapes=[
            pltpu.VMEM(TOKENS, BF16),
            pltpu.VMEM(TOKENS, BF16),
            pltpu.SemaphoreType.DMA((2, 2)),
        ],
    )
    return normed, qg, kg, vg


def solution(mesh):
    both = P("ctx", "head")
    return jax.shard_map(
        body,
        mesh=mesh,
        in_specs=(both, both, both, both, P("head"), P()),
        out_specs=(both, both, both, both),
        check_vma=False,
    )
```

```python
import functools

import jax
import jax.numpy as jnp
from jax import lax
from jax.experimental import pallas as pl
from jax.experimental.pallas import tpu as pltpu
from jax.sharding import PartitionSpec as P

DH = 128
BLK = 256
FEAT = 4096
EPSILON = 1e-06
TOK = 512
WIDE = 256
CHUNK = 512
GROUP = 16
F32 = jnp.float32
BF16 = jnp.bfloat16


def dot(a, b, ca, cb):
    return lax.dot_general(a, b, (((ca,), (cb,)), ((), ())), preferred_element_type=F32)


def iota(shape, dim):
    return lax.broadcasted_iota(jnp.int32, shape, dim).astype(F32)


def doc_starts(lengths_ref):
    docs = lengths_ref.shape[1]
    lengths = jnp.broadcast_to(lengths_ref[...].astype(F32), (docs, docs))
    i, j = iota((docs, docs), 0), iota((docs, docs), 1)
    column = jnp.sum(jnp.where(j < i, lengths, 0.0), axis=1, keepdims=True)
    return jnp.sum(jnp.where(i == j, column, 0.0), axis=0, keepdims=True)


def start_of(starts, positions):
    return jnp.max(jnp.where(starts <= positions, starts, 0.0), axis=1, keepdims=True)


def first_token():
    return (lax.axis_index("ctx") * TOK).astype(F32)


def span(b):
    return slice(b * BLK, (b + 1) * BLK)


def head(h):
    return slice(h * DH, (h + 1) * DH)


def diagonal(total):
    return [total[head(h), head(h)].reshape(8, 16, DH) for h in range(2)]


def summary_kernel(lengths_hbm, k_hbm, v_hbm, lengths_ref, k_ref, v_ref, out_ref, sems):
    parts = range(0, TOK, CHUNK)
    first = pltpu.make_async_copy(lengths_hbm, lengths_ref, sems.at[0])
    first.start()
    copies = []
    for n, at in enumerate(parts):
        rows = slice(at, at + CHUNK)
        for m, (hbm, ref) in enumerate(((k_hbm, k_ref), (v_hbm, v_ref))):
            copy = pltpu.make_async_copy(hbm.at[rows], ref.at[rows], sems.at[1 + 2 * n + m])
            copy.start()
            copies.append(copy)
    first.wait()
    starts = doc_starts(lengths_ref)
    last = jnp.broadcast_to(first_token() + (TOK - 1), (8, starts.shape[1]))
    start = start_of(starts, last)[:1] - first_token()
    total = 0.0
    for n, at in enumerate(parts):
        copies[2 * n].wait()
        copies[2 * n + 1].wait()
        rows = slice(at, at + CHUNK)
        open_end = (iota((CHUNK, WIDE), 0) + at >= start).astype(F32)
        k = (k_ref[rows].astype(F32) * open_end).astype(BF16)
        total = total + dot(k, v_ref[rows], 0, 0)
    for h, piece in enumerate(diagonal(total)):
        out_ref[h * 8 : (h + 1) * 8] = piece


def keeps(starts, reverse):
    group = lax.axis_index("ctx") // GROUP * GROUP
    left = (iota((GROUP, starts.shape[1]), 0) + group.astype(F32)) * TOK
    if reverse:
        return (start_of(starts, left + TOK) <= left[:, :1]).astype(F32)
    return (start_of(starts, left + (TOK - 1)) < left[:, :1]).astype(F32)


def order(reverse):
    return reversed(range(GROUP)) if reverse else range(GROUP)


def total_kernel(reverse, lengths_ref, x_ref, out_ref):
    keep = keeps(doc_starts(lengths_ref), reverse)
    now = jnp.zeros(out_ref.shape, F32)
    for i in order(reverse):
        now = x_ref[i] + keep[i : i + 1, :] * now
    out_ref[...] = now


def group_prefix(reverse, starts, x_ref, prefix_ref, open_ref):
    keep = keeps(starts, reverse)
    now = jnp.zeros(x_ref.shape[1:], F32)
    still = jnp.ones((1, DH), F32)
    for i in order(reverse):
        prefix_ref[i] = now
        open_ref[i : i + 1, :] = still
        now = x_ref[i] + keep[i : i + 1, :] * now
        still = keep[i : i + 1, :] * still


def join_kernel(prefix_ref, open_ref, before_ref, out_ref):
    before = before_ref[...]
    for i in range(GROUP):
        out_ref[i] = prefix_ref[i] + open_ref[i : i + 1, :] * before


def allowed(start_ref, b):
    start = start_ref[span(b), :] - (first_token() + b * BLK)
    start = jnp.concatenate([start, start], axis=1)
    t, s = iota((BLK, BLK), 0), iota((BLK, BLK), 1)
    return (s <= t) & (s >= start)


def within_kernel(
    lengths_ref,
    x_ref,
    q_ref,
    k_ref,
    v_ref,
    og_ref,
    gain_ref,
    prefix_ref,
    open_ref,
    start_ref,
    probs_ref,
    within_ref,
    scaled_ref,
    part_ref,
):
    starts = doc_starts(lengths_ref)
    group_prefix(False, starts, x_ref, prefix_ref, open_ref)
    positions = first_token() + iota((TOK + 8, starts.shape[1]), 0)
    start_ref[...] = jnp.broadcast_to(start_of(starts, positions), start_ref.shape)
    at = first_token() + iota((BLK, DH), 0)
    open_mid = (at >= start_ref[BLK - 1 : BLK, :]).astype(F32)
    for h in range(2):
        k = k_ref[:BLK, head(h)].astype(F32)
        part_ref[head(h), :] = dot((k * open_mid).astype(BF16), v_ref[:BLK, head(h)], 0, 0)
    for b in range(2):
        mask = allowed(start_ref, b)
        for h in range(2):
            where = (span(b), head(h))
            scores = dot(q_ref[where], k_ref[where], 1, 1)
            probs = jnp.where(mask, scores, 0.0).astype(BF16)
            probs_ref[2 * b + h] = probs
            within_ref[where] = dot(probs, v_ref[where], 1, 0)
            scaled_ref[where] = og_ref[where].astype(F32) * gain_ref[:, head(h)]


def both_heads(state):
    zero = jnp.zeros((DH, DH), F32)
    whole = jnp.concatenate(
        [
            jnp.concatenate([state[head(0)], zero], axis=1),
            jnp.concatenate([zero, state[head(1)]], axis=1),
        ],
        axis=0,
    )
    high = whole.astype(BF16)
    return high, (whole - high.astype(F32)).astype(BF16)


def dot_state(a, state, cs):
    return dot(a, state[0], 1, cs) + dot(a, state[1], 1, cs)


def entering(start_ref, state_ref, part_ref, b):
    state = state_ref[...]
    if b == 1:
        keep = (start_ref[BLK - 1 : BLK, :] < first_token()).astype(F32)
        state = keep * state + part_ref[...]
    return both_heads(state)


def twice(x):
    return jnp.concatenate([x, x], axis=1)


def applies_fwd(start_ref, b):
    return (start_ref[span(b), :] < first_token() + b * BLK).astype(F32)


def attend_kernel(
    start_ref, q_ref, scaled_ref, within_ref, state_ref, part_ref, att_ref, sums_ref
):
    rows = []
    for b in range(2):
        state = entering(start_ref, state_ref, part_ref, b)
        across = dot_state(q_ref[span(b)], state, 0)
        att = within_ref[span(b)] + across * twice(applies_fwd(start_ref, b))
        att_ref[span(b)] = att
        square, inner = att * att, scaled_ref[span(b)] * att
        rows.append((square[:, :DH] + square[:, DH:], inner[:, :DH] + inner[:, DH:]))
    lines = []
    for which in range(2):
        for b in range(2):
            for c in range(2):
                piece = rows[b][which][c * DH : (c + 1) * DH]
                lines.append(jnp.sum(piece.T, axis=0, keepdims=True))
    sums = jnp.concatenate(lines, axis=0)
    for i in range(16):
        sums_ref[i] = sums


def tall(row):
    return jnp.concatenate(
        [jnp.broadcast_to(row[c : c + 1, :], (DH, DH)).T for c in range(4)], axis=0
    )


def delta_kernel(start_ref, q_ref, scaled_ref, att_ref, sums_ref, delta_ref, out_ref):
    sums = jnp.sum(sums_ref[...], axis=0)
    radius = jnp.sqrt(sums[:4] / FEAT + EPSILON)
    inverse = twice(tall(1.0 / radius))
    factor = twice(tall(sums[4:] / (FEAT * radius * radius * radius)))
    open_start = twice((start_ref[:TOK, :] <= first_token()).astype(F32))
    delta = (scaled_ref[...] * inverse - att_ref[...] * factor).astype(BF16)
    delta_ref[...] = delta
    q = (q_ref[...].astype(F32) * open_start).astype(BF16)
    for h, piece in enumerate(diagonal(dot(q, delta, 0, 0))):
        out_ref[h * 8 : (h + 1) * 8] = piece


def local_grads_kernel(
    lengths_ref,
    start_ref,
    x_ref,
    q_ref,
    k_ref,
    v_ref,
    gain_ref,
    att_ref,
    delta_ref,
    sums_ref,
    probs_ref,
    state_ref,
    part_ref,
    prefix_ref,
    open_ref,
    normed_ref,
    qg_ref,
    kg_ref,
    vg_ref,
    back_ref,
):
    group_prefix(True, doc_starts(lengths_ref), x_ref, prefix_ref, open_ref)
    sums = jnp.sum(sums_ref[...], axis=0)
    inverse = tall(1.0 / jnp.sqrt(sums[:4] / FEAT + EPSILON))
    open_mid = (start_ref[span(1), :] <= first_token() + BLK).astype(F32)
    for h in range(2):
        q = q_ref[BLK:, head(h)].astype(F32)
        back_ref[head(h), :] = dot((q * open_mid).astype(BF16), delta_ref[BLK:, head(h)], 0, 0)
    for b in range(2):
        mask = allowed(start_ref, b)
        apply = twice(applies_fwd(start_ref, b))
        state = entering(start_ref, state_ref, part_ref, b)
        across = dot_state(delta_ref[span(b)], state, 1) * apply
        for h in range(2):
            where = (span(b), head(h))
            normed_ref[where] = (att_ref[where] * inverse[span(b)] * gain_ref[:, head(h)]).astype(
                BF16
            )
            delta = delta_ref[where]
            dprobs = jnp.where(mask, dot(delta, v_ref[where], 1, 1), 0.0).astype(BF16)
            qg_ref[where] = (dot(dprobs, k_ref[where], 1, 0) + across[:, head(h)]).astype(BF16)
            kg_ref[where] = dot(dprobs, q_ref[where], 0, 0)
            vg_ref[where] = dot(probs_ref[2 * b + h], delta, 0, 0)


def last_grads_kernel(
    start_ref,
    k_ref,
    v_ref,
    kg_in_ref,
    vg_in_ref,
    state_ref,
    part_ref,
    kg_hbm,
    vg_hbm,
    kg_ref,
    vg_ref,
    sems,
):
    base = first_token()
    keep = (start_ref[TOK : TOK + 1, :] <= base + BLK).astype(F32)
    state = state_ref[...]
    states = [both_heads(keep * state + part_ref[...]), both_heads(state)]
    applies = []
    for b in range(2):
        edge = (b + 1) * BLK
        at = base + b * BLK + iota((BLK, DH), 0)
        applies.append(twice((at >= start_ref[edge : edge + 1, :]).astype(F32)))
    copies = []
    for i, (local, x, side, ref, hbm) in enumerate(
        ((kg_in_ref, v_ref, 1, kg_ref, kg_hbm), (vg_in_ref, k_ref, 0, vg_ref, vg_hbm))
    ):
        for b in range(2):
            across = dot_state(x[span(b)], states[b], side) * applies[b]
            ref[span(b)] = (local[span(b)] + across).astype(BF16)
        copy = pltpu.make_async_copy(ref, hbm, sems.at[i])
        copy.start()
        copies.append(copy)
    for copy in copies:
        copy.wait()


def call(kernel, outs, *args, flops=0, name=None, grant=24, bound=True, **rest):
    shapes = [jax.ShapeDtypeStruct(s, d) for s, d in outs]
    moved = sum(a.size * a.dtype.itemsize for a in args)
    moved += sum(s.size * s.dtype.itemsize for s in shapes)
    moved = moved if bound else 0
    return pl.pallas_call(
        kernel,
        out_shape=shapes,
        compiler_params=pltpu.CompilerParams(vmem_limit_bytes=grant << 20),
        cost_estimate=pl.CostEstimate(flops=flops, bytes_accessed=moved, transcendentals=0),
        name=name,
        **rest,
    )(*args)


HBM = pl.BlockSpec(memory_space=pltpu.HBM)
VMEM = pl.BlockSpec(memory_space=pltpu.VMEM)
TOKENS = (TOK, WIDE)
STATES = (2 * DH, DH)
PIECE = (GROUP, DH)
PIECES = (GROUP, GROUP, DH)


def swap(x):
    count = lax.axis_size("ctx")
    groups = [list(range(g, g + GROUP)) for g in range(0, count, GROUP)]
    return lax.all_to_all(x, "ctx", 0, 0, axis_index_groups=groups)


def total_before(lengths, x, reverse):
    step = -GROUP if reverse else GROUP
    count = lax.axis_size("ctx")
    pairs = [(i, i + step) for i in range(count) if 0 <= i + step < count]
    kernel = functools.partial(total_kernel, reverse)
    (total,) = call(kernel, [(PIECE, F32)], lengths, x, name="total")
    return lax.ppermute(total, "ctx", pairs)


def joined(prefix, still, before):
    (y,) = call(join_kernel, [(PIECES, F32)], prefix, still, before, name="join")
    return swap(y).reshape(STATES)


def body(q, k, v, og, gain, lengths):
    lengths = lengths.reshape(1, -1)
    gain = gain.reshape(1, -1)
    docs = lengths.shape
    lengths, k, v, summary = call(
        summary_kernel,
        [(docs, jnp.int32), (TOKENS, BF16), (TOKENS, BF16), (PIECES, F32)],
        *(pltpu.with_memory_space_constraint(a, pltpu.HBM) for a in (lengths, k, v)),
        flops=1 << 26,
        name="summary",
        in_specs=[HBM] * 3,
        scratch_shapes=[pltpu.SemaphoreType.DMA((1 + 2 * (TOK // CHUNK),))],
    )
    q, og, summary = lax.optimization_barrier((q, og, summary))
    x = swap(summary)
    before = total_before(lengths, x, False)
    prefix, still, start, probs, within, scaled, part = call(
        within_kernel,
        [
            (PIECES, F32),
            (PIECE, F32),
            ((TOK + 8, DH), F32),
            ((4, BLK, BLK), BF16),
            (TOKENS, F32),
            (TOKENS, F32),
            (STATES, F32),
        ],
        lengths,
        x,
        q,
        k,
        v,
        og,
        gain,
        flops=1 << 28,
        name="within",
    )
    state = joined(prefix, still, before)
    att, sums = call(
        attend_kernel,
        [(TOKENS, F32), ((16, 8, DH), F32)],
        start,
        q,
        scaled,
        within,
        state,
        part,
        flops=1 << 27,
        name="attend",
    )
    sums = lax.all_to_all(sums, "head", 0, 0)
    delta, summary = call(
        delta_kernel,
        [(TOKENS, BF16), (PIECES, F32)],
        start,
        q,
        scaled,
        att,
        sums,
        flops=1 << 26,
        name="delta",
    )
    x = swap(summary)
    before = total_before(lengths, x, True)
    prefix, still, normed, qg, kg, vg, part_back = call(
        local_grads_kernel,
        [
            (PIECES, F32),
            (PIECE, F32),
            (TOKENS, BF16),
            (TOKENS, BF16),
            (TOKENS, F32),
            (TOKENS, F32),
            (STATES, F32),
        ],
        lengths,
        start,
        x,
        q,
        k,
        v,
        gain,
        att,
        delta,
        sums,
        probs,
        state,
        part,
        flops=1 << 29,
        name="local_grads",
    )
    state_back = joined(prefix, still, before)
    kg, vg = call(
        last_grads_kernel,
        [(TOKENS, BF16), (TOKENS, BF16)],
        start,
        k,
        v,
        kg,
        vg,
        state_back,
        part_back,
        flops=1 << 28,
        name="last_grads",
        in_specs=[VMEM] * 7,
        out_specs=[HBM] * 2,
        scratch_shapes=[
            pltpu.VMEM(TOKENS, BF16),
            pltpu.VMEM(TOKENS, BF16),
            pltpu.SemaphoreType.DMA((2,)),
        ],
    )
    return normed, qg, kg, vg


def solution(mesh):
    both = P("ctx", "head")
    return jax.shard_map(
        body,
        mesh=mesh,
        in_specs=(both, both, both, both, P("head"), P()),
        out_specs=(both, both, both, both),
        check_vma=False,
    )
```

```python
import functools

import jax
import jax.numpy as jnp
from jax import lax
from jax.experimental import pallas as pl
from jax.experimental.pallas import tpu as pltpu
from jax.sharding import PartitionSpec as P

DH = 128
BLK = 256
FEAT = 4096
EPSILON = 1e-06
TOK = 512
WIDE = 256
CHUNK = 512
GROUP = 16
F32 = jnp.float32
BF16 = jnp.bfloat16


def dot(a, b, ca, cb):
    return lax.dot_general(a, b, (((ca,), (cb,)), ((), ())), preferred_element_type=F32)


def iota(shape, dim):
    return lax.broadcasted_iota(jnp.int32, shape, dim).astype(F32)


def doc_starts(lengths_ref):
    docs = lengths_ref.shape[1]
    lengths = jnp.broadcast_to(lengths_ref[...].astype(F32), (docs, docs))
    i, j = iota((docs, docs), 0), iota((docs, docs), 1)
    column = jnp.sum(jnp.where(j < i, lengths, 0.0), axis=1, keepdims=True)
    return jnp.sum(jnp.where(i == j, column, 0.0), axis=0, keepdims=True)


def start_of(starts, positions):
    return jnp.max(jnp.where(starts <= positions, starts, 0.0), axis=1, keepdims=True)


def first_token():
    return (lax.axis_index("ctx") * TOK).astype(F32)


def span(b):
    return slice(b * BLK, (b + 1) * BLK)


def head(h):
    return slice(h * DH, (h + 1) * DH)


def diagonal(total):
    return [total[head(h), head(h)].reshape(8, 16, DH) for h in range(2)]


def summary_kernel(lengths_hbm, k_hbm, v_hbm, lengths_ref, k_ref, v_ref, out_ref, sems):
    parts = range(0, TOK, CHUNK)
    first = pltpu.make_async_copy(lengths_hbm, lengths_ref, sems.at[0])
    first.start()
    copies = []
    for n, at in enumerate(parts):
        rows = slice(at, at + CHUNK)
        for m, (hbm, ref) in enumerate(((k_hbm, k_ref), (v_hbm, v_ref))):
            copy = pltpu.make_async_copy(hbm.at[rows], ref.at[rows], sems.at[1 + 2 * n + m])
            copy.start()
            copies.append(copy)
    first.wait()
    starts = doc_starts(lengths_ref)
    last = jnp.broadcast_to(first_token() + (TOK - 1), (8, starts.shape[1]))
    start = start_of(starts, last)[:1] - first_token()
    total = 0.0
    for n, at in enumerate(parts):
        copies[2 * n].wait()
        copies[2 * n + 1].wait()
        rows = slice(at, at + CHUNK)
        open_end = (iota((CHUNK, WIDE), 0) + at >= start).astype(F32)
        k = (k_ref[rows].astype(F32) * open_end).astype(BF16)
        total = total + dot(k, v_ref[rows], 0, 0)
    for h, piece in enumerate(diagonal(total)):
        out_ref[h * 8 : (h + 1) * 8] = piece


def keeps(starts, reverse):
    group = lax.axis_index("ctx") // GROUP * GROUP
    left = (iota((GROUP, starts.shape[1]), 0) + group.astype(F32)) * TOK
    if reverse:
        return (start_of(starts, left + TOK) <= left[:, :1]).astype(F32)
    return (start_of(starts, left + (TOK - 1)) < left[:, :1]).astype(F32)


def order(reverse):
    return reversed(range(GROUP)) if reverse else range(GROUP)


def total_kernel(reverse, lengths_ref, x_ref, out_ref):
    keep = keeps(doc_starts(lengths_ref), reverse)
    now = jnp.zeros(out_ref.shape, F32)
    for i in order(reverse):
        now = x_ref[i] + keep[i : i + 1, :] * now
    out_ref[...] = now


def group_prefix(reverse, starts, x_ref, prefix_ref, open_ref):
    keep = keeps(starts, reverse)
    now = jnp.zeros(x_ref.shape[1:], F32)
    still = jnp.ones((1, DH), F32)
    for i in order(reverse):
        prefix_ref[i] = now
        open_ref[i : i + 1, :] = still
        now = x_ref[i] + keep[i : i + 1, :] * now
        still = keep[i : i + 1, :] * still


def join_kernel(prefix_ref, open_ref, before_ref, out_ref):
    before = before_ref[...]
    for i in range(GROUP):
        out_ref[i] = prefix_ref[i] + open_ref[i : i + 1, :] * before


def allowed(start_ref, b):
    start = start_ref[span(b), :] - (first_token() + b * BLK)
    start = jnp.concatenate([start, start], axis=1)
    t, s = iota((BLK, BLK), 0), iota((BLK, BLK), 1)
    return (s <= t) & (s >= start)


def within_kernel(
    lengths_ref,
    x_ref,
    q_ref,
    k_ref,
    v_ref,
    og_hbm,
    gain_hbm,
    prefix_ref,
    open_ref,
    start_ref,
    probs_ref,
    within_ref,
    scaled_ref,
    part_ref,
    og_ref,
    gain_ref,
    sems,
):
    copies = [
        pltpu.make_async_copy(og_hbm, og_ref, sems.at[0]),
        pltpu.make_async_copy(gain_hbm, gain_ref, sems.at[1]),
    ]
    for copy in copies:
        copy.start()
    starts = doc_starts(lengths_ref)
    group_prefix(False, starts, x_ref, prefix_ref, open_ref)
    positions = first_token() + iota((TOK + 8, starts.shape[1]), 0)
    start_ref[...] = jnp.broadcast_to(start_of(starts, positions), start_ref.shape)
    at = first_token() + iota((BLK, DH), 0)
    open_mid = (at >= start_ref[BLK - 1 : BLK, :]).astype(F32)
    for h in range(2):
        k = k_ref[:BLK, head(h)].astype(F32)
        part_ref[head(h), :] = dot((k * open_mid).astype(BF16), v_ref[:BLK, head(h)], 0, 0)
    for b in range(2):
        mask = allowed(start_ref, b)
        for h in range(2):
            where = (span(b), head(h))
            scores = dot(q_ref[where], k_ref[where], 1, 1)
            probs = jnp.where(mask, scores, 0.0).astype(BF16)
            probs_ref[2 * b + h] = probs
            within_ref[where] = dot(probs, v_ref[where], 1, 0)
    for copy in copies:
        copy.wait()
    scaled_ref[...] = og_ref[...].astype(F32) * gain_ref[...]


def both_heads(state):
    zero = jnp.zeros((DH, DH), F32)
    whole = jnp.concatenate(
        [
            jnp.concatenate([state[head(0)], zero], axis=1),
            jnp.concatenate([zero, state[head(1)]], axis=1),
        ],
        axis=0,
    )
    high = whole.astype(BF16)
    return high, (whole - high.astype(F32)).astype(BF16)


def dot_state(a, state, cs):
    return dot(a, state[0], 1, cs) + dot(a, state[1], 1, cs)


def entering(start_ref, state_ref, part_ref, b):
    state = state_ref[...]
    if b == 1:
        keep = (start_ref[BLK - 1 : BLK, :] < first_token()).astype(F32)
        state = keep * state + part_ref[...]
    return both_heads(state)


def twice(x):
    return jnp.concatenate([x, x], axis=1)


def applies_fwd(start_ref, b):
    return (start_ref[span(b), :] < first_token() + b * BLK).astype(F32)


def attend_kernel(
    start_ref, q_ref, scaled_ref, within_ref, state_ref, part_ref, att_ref, sums_ref
):
    rows = []
    for b in range(2):
        state = entering(start_ref, state_ref, part_ref, b)
        across = dot_state(q_ref[span(b)], state, 0)
        att = within_ref[span(b)] + across * twice(applies_fwd(start_ref, b))
        att_ref[span(b)] = att
        square, inner = att * att, scaled_ref[span(b)] * att
        rows.append((square[:, :DH] + square[:, DH:], inner[:, :DH] + inner[:, DH:]))
    lines = []
    for which in range(2):
        for b in range(2):
            for c in range(2):
                piece = rows[b][which][c * DH : (c + 1) * DH]
                lines.append(jnp.sum(piece.T, axis=0, keepdims=True))
    sums = jnp.concatenate(lines, axis=0)
    for i in range(16):
        sums_ref[i] = sums


def tall(row):
    return jnp.concatenate(
        [jnp.broadcast_to(row[c : c + 1, :], (DH, DH)).T for c in range(4)], axis=0
    )


def delta_kernel(start_ref, q_ref, scaled_ref, att_ref, sums_ref, delta_ref, out_ref):
    sums = jnp.sum(sums_ref[...], axis=0)
    radius = jnp.sqrt(sums[:4] / FEAT + EPSILON)
    inverse = twice(tall(1.0 / radius))
    factor = twice(tall(sums[4:] / (FEAT * radius * radius * radius)))
    open_start = twice((start_ref[:TOK, :] <= first_token()).astype(F32))
    delta = (scaled_ref[...] * inverse - att_ref[...] * factor).astype(BF16)
    delta_ref[...] = delta
    q = (q_ref[...].astype(F32) * open_start).astype(BF16)
    for h, piece in enumerate(diagonal(dot(q, delta, 0, 0))):
        out_ref[h * 8 : (h + 1) * 8] = piece


def local_grads_kernel(
    lengths_ref,
    start_ref,
    x_ref,
    q_ref,
    k_ref,
    v_ref,
    gain_ref,
    att_ref,
    delta_ref,
    sums_ref,
    probs_ref,
    state_ref,
    part_ref,
    prefix_ref,
    open_ref,
    normed_ref,
    qg_ref,
    kg_ref,
    vg_ref,
    back_ref,
):
    group_prefix(True, doc_starts(lengths_ref), x_ref, prefix_ref, open_ref)
    sums = jnp.sum(sums_ref[...], axis=0)
    inverse = tall(1.0 / jnp.sqrt(sums[:4] / FEAT + EPSILON))
    open_mid = (start_ref[span(1), :] <= first_token() + BLK).astype(F32)
    for h in range(2):
        q = q_ref[BLK:, head(h)].astype(F32)
        back_ref[head(h), :] = dot((q * open_mid).astype(BF16), delta_ref[BLK:, head(h)], 0, 0)
    for b in range(2):
        mask = allowed(start_ref, b)
        apply = twice(applies_fwd(start_ref, b))
        state = entering(start_ref, state_ref, part_ref, b)
        across = dot_state(delta_ref[span(b)], state, 1) * apply
        for h in range(2):
            where = (span(b), head(h))
            normed_ref[where] = (att_ref[where] * inverse[span(b)] * gain_ref[:, head(h)]).astype(
                BF16
            )
            delta = delta_ref[where]
            dprobs = jnp.where(mask, dot(delta, v_ref[where], 1, 1), 0.0).astype(BF16)
            qg_ref[where] = (dot(dprobs, k_ref[where], 1, 0) + across[:, head(h)]).astype(BF16)
            kg_ref[where] = dot(dprobs, q_ref[where], 0, 0)
            vg_ref[where] = dot(probs_ref[2 * b + h], delta, 0, 0)


def last_grads_kernel(
    start_ref,
    k_ref,
    v_ref,
    kg_in_ref,
    vg_in_ref,
    state_ref,
    part_ref,
    kg_hbm,
    vg_hbm,
    kg_ref,
    vg_ref,
    sems,
):
    base = first_token()
    keep = (start_ref[TOK : TOK + 1, :] <= base + BLK).astype(F32)
    state = state_ref[...]
    states = [both_heads(keep * state + part_ref[...]), both_heads(state)]
    applies = []
    for b in range(2):
        edge = (b + 1) * BLK
        at = base + b * BLK + iota((BLK, DH), 0)
        applies.append(twice((at >= start_ref[edge : edge + 1, :]).astype(F32)))
    copies = []
    for i, (local, x, side, ref, hbm) in enumerate(
        ((kg_in_ref, v_ref, 1, kg_ref, kg_hbm), (vg_in_ref, k_ref, 0, vg_ref, vg_hbm))
    ):
        for b in range(2):
            across = dot_state(x[span(b)], states[b], side) * applies[b]
            ref[span(b)] = (local[span(b)] + across).astype(BF16)
        copy = pltpu.make_async_copy(ref, hbm, sems.at[i])
        copy.start()
        copies.append(copy)
    for copy in copies:
        copy.wait()


def call(kernel, outs, *args, flops=0, name=None, grant=24, bound=True, **rest):
    shapes = [jax.ShapeDtypeStruct(s, d) for s, d in outs]
    moved = sum(a.size * a.dtype.itemsize for a in args)
    moved += sum(s.size * s.dtype.itemsize for s in shapes)
    moved = moved if bound else 0
    return pl.pallas_call(
        kernel,
        out_shape=shapes,
        compiler_params=pltpu.CompilerParams(vmem_limit_bytes=grant << 20),
        cost_estimate=pl.CostEstimate(flops=flops, bytes_accessed=moved, transcendentals=0),
        name=name,
        **rest,
    )(*args)


HBM = pl.BlockSpec(memory_space=pltpu.HBM)
VMEM = pl.BlockSpec(memory_space=pltpu.VMEM)
TOKENS = (TOK, WIDE)
STATES = (2 * DH, DH)
PIECE = (GROUP, DH)
PIECES = (GROUP, GROUP, DH)


def swap(x):
    count = lax.axis_size("ctx")
    groups = [list(range(g, g + GROUP)) for g in range(0, count, GROUP)]
    return lax.all_to_all(x, "ctx", 0, 0, axis_index_groups=groups)


def total_before(lengths, x, reverse):
    step = -GROUP if reverse else GROUP
    count = lax.axis_size("ctx")
    pairs = [(i, i + step) for i in range(count) if 0 <= i + step < count]
    kernel = functools.partial(total_kernel, reverse)
    (total,) = call(kernel, [(PIECE, F32)], lengths, x, name="total")
    return lax.ppermute(total, "ctx", pairs)


def joined(prefix, still, before):
    (y,) = call(join_kernel, [(PIECES, F32)], prefix, still, before, name="join")
    return swap(y).reshape(STATES)


def body(q, k, v, og, gain, lengths):
    lengths = lengths.reshape(1, -1)
    gain = gain.reshape(1, -1)
    docs = lengths.shape
    lengths, k, v, summary = call(
        summary_kernel,
        [(docs, jnp.int32), (TOKENS, BF16), (TOKENS, BF16), (PIECES, F32)],
        *(pltpu.with_memory_space_constraint(a, pltpu.HBM) for a in (lengths, k, v)),
        flops=1 << 26,
        name="summary",
        in_specs=[HBM] * 3,
        scratch_shapes=[pltpu.SemaphoreType.DMA((1 + 2 * (TOK // CHUNK),))],
    )
    q, og, summary = lax.optimization_barrier((q, og, summary))
    x = swap(summary)
    before = total_before(lengths, x, False)
    prefix, still, start, probs, within, scaled, part = call(
        within_kernel,
        [
            (PIECES, F32),
            (PIECE, F32),
            ((TOK + 8, DH), F32),
            ((4, BLK, BLK), BF16),
            (TOKENS, F32),
            (TOKENS, F32),
            (STATES, F32),
        ],
        lengths,
        x,
        q,
        k,
        v,
        *(pltpu.with_memory_space_constraint(a, pltpu.HBM) for a in (og, gain)),
        flops=1 << 28,
        name="within",
        in_specs=[VMEM] * 5 + [HBM] * 2,
        scratch_shapes=[
            pltpu.VMEM(TOKENS, BF16),
            pltpu.VMEM((1, WIDE), F32),
            pltpu.SemaphoreType.DMA((2,)),
        ],
    )
    state = joined(prefix, still, before)
    att, sums = call(
        attend_kernel,
        [(TOKENS, F32), ((16, 8, DH), F32)],
        start,
        q,
        scaled,
        within,
        state,
        part,
        flops=1 << 27,
        name="attend",
    )
    sums = lax.all_to_all(sums, "head", 0, 0)
    delta, summary = call(
        delta_kernel,
        [(TOKENS, BF16), (PIECES, F32)],
        start,
        q,
        scaled,
        att,
        sums,
        flops=1 << 26,
        name="delta",
    )
    x = swap(summary)
    before = total_before(lengths, x, True)
    prefix, still, normed, qg, kg, vg, part_back = call(
        local_grads_kernel,
        [
            (PIECES, F32),
            (PIECE, F32),
            (TOKENS, BF16),
            (TOKENS, BF16),
            (TOKENS, F32),
            (TOKENS, F32),
            (STATES, F32),
        ],
        lengths,
        start,
        x,
        q,
        k,
        v,
        gain,
        att,
        delta,
        sums,
        probs,
        state,
        part,
        flops=1 << 29,
        name="local_grads",
    )
    state_back = joined(prefix, still, before)
    kg, vg = call(
        last_grads_kernel,
        [(TOKENS, BF16), (TOKENS, BF16)],
        start,
        k,
        v,
        kg,
        vg,
        state_back,
        part_back,
        flops=1 << 28,
        name="last_grads",
        in_specs=[VMEM] * 7,
        out_specs=[HBM] * 2,
        scratch_shapes=[
            pltpu.VMEM(TOKENS, BF16),
            pltpu.VMEM(TOKENS, BF16),
            pltpu.SemaphoreType.DMA((2,)),
        ],
    )
    return normed, qg, kg, vg


def solution(mesh):
    both = P("ctx", "head")
    return jax.shard_map(
        body,
        mesh=mesh,
        in_specs=(both, both, both, both, P("head"), P()),
        out_specs=(both, both, both, both),
        check_vma=False,
    )
```
